256 devices in a mesh: outer: 16 (over z, x_hi), inner: 16 (over x_lo, y, core).
Axes of the slice: x: 4 (x_hi: 2, x_lo: 2; x = x_hi * 2 + x_lo), y: 4, z: 8, core: 2. Of those that a mesh axis runs over, the one named last changes fastest.
Arguments:
- resid: bfloat16 [32768, 2048], P(('outer', 'inner')), may hold values from -40 to 40
- queries: bfloat16 [32768, 256], P(('outer', 'inner')), may hold values from -80 to 80
- keyvals: bfloat16 [32768, 256], P(('outer', 'inner')), may hold values from -10 to 10
- piece_order: int32 [32], replicated, may hold values from 0 to 31, each once
- out_proj: bfloat16 [256, 2048], replicated, may hold values from -0.75 to 0.75
- mlp_gain: float32 [2048], replicated, may hold values from 0.25 to 1.75
- w_gate: bfloat16 [2048, 7168], P('inner', 'outer'), may hold values from -0.125 to 0.125
- w_up: bfloat16 [2048, 7168], P('inner', 'outer'), may hold values from -0.125 to 0.125
- w_down: bfloat16 [7168, 2048], P('outer', 'inner'), may hold values from -0.0625 to 0.0625
Outputs:
- layer_out: bfloat16 [32768, 2048], P(('outer', 'inner'))
The draws below stay inside these ranges and needn't reach their ends.
Inputs may be any that keep to these rules, and one draw needn't show every extreme that they name: `piece_order`: each of the 32 piece numbers appears once.
All inputs are finite; a program needn't handle non-finite values.
Results may differ from the reference program's by a relative error of at most 0.014.
Values may be sent and summed in bfloat16 or wider, within the bound.
No kernel may reach another device: no remote copies, remote signals or barrier semaphores. Data moves between devices by JAX's collectives and lax.ppermute only.
A program may use at most 64 MiB of HBM per device.

```python
import jax
import jax.numpy as jnp
from jax import lax

D = 2048
FF = 7168
HD = 128
QHEADS = 2
SPAN = 64
PIECES = 32
BLOCK = 2048
SEQ = 32768


def attention_inputs(key):
    base_key = jax.random.fold_in(key, 7)
    query_key, key_key, value_key = jax.random.split(base_key, 3)
    queries = jnp.clip(jax.random.normal(query_key, (SEQ, QHEADS * HD), jnp.float32), -4.0, 4.0)
    key_rows = 2.5 * jnp.clip(jax.random.normal(key_key, (SEQ, HD), jnp.float32), -4.0, 4.0)
    values = jnp.clip(jax.random.normal(value_key, (SEQ, HD), jnp.float32), -4.0, 4.0)
    return (queries, jnp.concatenate([key_rows, values], 1))


def draw_queries(key, part):
    return attention_inputs(key)[0].astype(jnp.bfloat16)


def draw_keyvals(key, part):
    return attention_inputs(key)[1].astype(jnp.bfloat16)


def draw_resid(key, part):
    base_key = jax.random.fold_in(key, 11)
    normal_key = jax.random.fold_in(base_key, 0)
    values = jnp.clip(jax.random.normal(normal_key, (SEQ, D), jnp.float32), -4.0, 4.0)
    return values.astype(jnp.bfloat16)


def block_scale(rng, extent, shards, low, top_value):
    gain, own = 1.0, jax.random.fold_in(rng, 6)
    for dim, parts in shards:
        draws = jnp.exp(jax.random.uniform(jax.random.fold_in(own, dim), (parts,), jnp.float32, low / len(shards), top_value / len(shards)))
        gain = gain * jnp.repeat(draws, extent[dim] // parts).reshape([-1 if axis == dim else 1 for axis in range(len(extent))])
    return gain


def scatter_about(rng, extent, scale, reach, cuts=(), held_as=jnp.bfloat16):
    gain = block_scale(rng, extent, cuts, -0.22, 0.18) if cuts else 1.0
    entries = jax.random.normal(rng, extent, jnp.float32) * scale * gain
    return jnp.minimum(jnp.maximum(entries, -reach), reach).astype(held_as)


def setup_inputs(seed: int = 0) -> dict:
    streams_of = jax.random.split(jax.random.key(seed), 10)
    return {
        "resid": draw_resid(jax.random.fold_in(streams_of[9], 71), 0),
        "queries": draw_queries(jax.random.fold_in(streams_of[9], 71), 0),
        "keyvals": draw_keyvals(jax.random.fold_in(streams_of[9], 71), 0),
        "piece_order": jax.random.permutation(streams_of[3], PIECES).astype(jnp.int32),
        "out_proj": scatter_about(streams_of[4], (QHEADS * HD, D), 64 ** -0.5, 0.75),
        "mlp_gain": jnp.clip(1.0 + 0.15 * jax.random.normal(streams_of[5], (D,), jnp.float32), 0.25, 1.75),
        "w_gate": scatter_about(streams_of[6], (D, FF), D ** -0.5, 0.125, ((0, 16), (1, 16))),
        "w_up": scatter_about(streams_of[7], (D, FF), D ** -0.5, 0.125, ((0, 16), (1, 16))),
        "w_down": scatter_about(streams_of[8], (FF, D), FF ** -0.5, 0.0625, ((0, 16), (1, 16))),
    }


def reference(resid, queries, keyvals, piece_order, out_proj, mlp_gain, w_gate, w_up, w_down):
    block_pos = (piece_order[:, None] * SPAN + jnp.arange(SPAN, dtype=jnp.int32)[None, :]).reshape(BLOCK)
    block_count = SEQ // BLOCK
    query_blocks = queries.reshape(block_count, BLOCK, QHEADS, HD)
    kv_blocks = keyvals.reshape(block_count, BLOCK, 2 * HD)
    before_blocks = jnp.concatenate([jnp.zeros_like(kv_blocks[:1]), kv_blocks[:-1]], 0)
    score_scale = HD ** (-0.5)

    def one_block(inputs):
        query_part, own_part, before_part, block_id = inputs
        key_rows = jnp.concatenate([own_part[:, :HD], before_part[:, :HD]], 0)
        value_rows = jnp.concatenate([own_part[:, HD:], before_part[:, HD:]], 0)
        scores = jnp.einsum('thd,kd->htk', query_part.astype(jnp.float32), key_rows.astype(jnp.float32)) * score_scale
        own_visible = block_pos[None, :] <= block_pos[:, None]
        before_visible = jnp.broadcast_to(block_id > 0, (BLOCK, BLOCK))
        visible = jnp.concatenate([own_visible, before_visible], 1)
        scores = jnp.where(visible[None], scores, -jnp.inf)
        top_score = lax.optimization_barrier(jnp.max(scores, axis=-1, keepdims=True))
        weights = jnp.where(visible[None], jnp.exp(scores - top_score), 0.0)
        totals = lax.optimization_barrier(jnp.sum(weights, axis=-1, keepdims=True))
        probs = weights.astype(jnp.bfloat16)
        mixed = jnp.einsum('htk,kd->htd', probs.astype(jnp.float32), value_rows.astype(jnp.float32)) / totals
        return mixed.transpose(1, 0, 2).reshape(BLOCK, QHEADS * HD).astype(jnp.bfloat16)
    attended = lax.map(one_block, (query_blocks, kv_blocks, before_blocks, jnp.arange(block_count, dtype=jnp.int32)))
    attended = attended.reshape(SEQ, QHEADS * HD)
    after_attn = (resid.astype(jnp.float32) + jnp.dot(attended, out_proj, preferred_element_type=jnp.float32)).astype(jnp.bfloat16)

    def mlp_block(rows_in):
        after_wide = rows_in.astype(jnp.float32)
        normed = (after_wide * lax.rsqrt(lax.optimization_barrier(jnp.mean(after_wide * after_wide, axis=-1, keepdims=True)) + 1e-05) * mlp_gain).astype(jnp.bfloat16)
        gate = jnp.dot(normed, w_gate, preferred_element_type=jnp.float32)
        upward = jnp.dot(normed, w_up, preferred_element_type=jnp.float32)
        hidden = (jax.nn.silu(gate) * upward).astype(jnp.bfloat16)
        mlp_sum = jnp.dot(hidden, w_down, preferred_element_type=jnp.float32)
        return (after_wide + mlp_sum).astype(jnp.bfloat16)
    layer_out = lax.map(mlp_block, after_attn.reshape(block_count, BLOCK, D))
    return layer_out.reshape(SEQ, D)
```

```python
import functools

import jax
import jax.numpy as jnp
from jax import lax
from jax.experimental import pallas as pl
from jax.experimental.pallas import tpu as pltpu
from jax.sharding import PartitionSpec as P

HD = 128
QHEADS = 2
SPAN = 64
AXES = ("outer", "inner")
F32 = jnp.float32
BF16 = jnp.bfloat16


def device_at(z, x, y, core):
    return ((z * 2 + x // 2) * 2 + x % 2) * 8 + y * 2 + core


def places():
    return [(z, x, y, core) for z in range(8) for x in range(4) for y in range(4) for core in range(2)]


def z_step(array, distance):
    route = [
        (device_at(z, x, y, core), device_at((z + distance) % 8, x, y, core))
        for z, x, y, core in places()
    ]
    return lax.ppermute(array, AXES, route)


def other_core(array):
    route = [
        (device_at(z, x, y, core), device_at(z, x, y, 1 - core)) for z, x, y, core in places()
    ]
    return lax.ppermute(array, AXES, route)


def from_previous_block(array):
    count = 16
    route = [((o - 1) % count * 16 + i, o * 16 + i) for o in range(count) for i in range(16)]
    return lax.ppermute(array, AXES, route)


def attention_kernel(has_before, q_ref, own_ref, sib_ref, qpos_ref, kpos_ref, out_ref):
    rows = q_ref.shape[0]
    q = jnp.concatenate([q_ref[:, :HD], q_ref[:, HD:]], axis=0)
    qpos = jnp.concatenate([qpos_ref[...], qpos_ref[...]], axis=0)
    scores, values, seen = [], [], []
    for part, ref in enumerate((own_ref, sib_ref)):
        keys = ref.shape[0] * ref.shape[1]
        kv = ref[...].reshape(keys, ref.shape[2])
        for before in range(2):
            base = before * 2 * HD
            score = lax.dot_general(
                q, kv[:, base : base + HD], (((1,), (1,)), ((), ())), preferred_element_type=F32
            ) * HD ** (-0.5)
            if before:
                visible = jnp.broadcast_to(has_before[0] > 0, score.shape)
            else:
                visible = kpos_ref[part : part + 1, :] <= qpos
            scores.append(jnp.where(visible, score, -1e30))
            seen.append(visible)
            values.append(kv[:, base + HD : base + 2 * HD])
    top = functools.reduce(jnp.maximum, [jnp.max(s, axis=1, keepdims=True) for s in scores])
    total = jnp.zeros((q.shape[0], 1), F32)
    mixed = jnp.zeros((q.shape[0], HD), F32)
    for score, visible, value in zip(scores, seen, values):
        weight = jnp.where(visible, jnp.exp(score - top), 0.0)
        total = total + jnp.sum(weight, axis=1, keepdims=True)
        mixed = mixed + jnp.dot(weight.astype(BF16), value, preferred_element_type=F32)
    attended = (mixed / total).astype(BF16)
    attended = jnp.concatenate([attended[:rows], attended[rows:]], axis=1)
    for copy in range(out_ref.shape[0]):
        out_ref[copy] = attended


def mlp_kernel(distances, with_after, z_ref, *refs):
    count = len(distances)
    resid_refs = refs[: 2 * count]
    att_ref, proj_ref, gain_ref, gate_ref, up_ref, down_ref = refs[2 * count : 2 * count + 6]
    rest = refs[2 * count + 6 :]
    out_refs = rest[: 2 * count]
    after_ref = rest[2 * count] if with_after else None
    normed_ref, total_ref = rest[-2:]
    step = pl.program_id(0)
    half = resid_refs[0].shape[0]

    @pl.when(step == 0)
    def _():
        for n, distance in enumerate(distances):
            mixed = jnp.dot(
                att_ref[lax.rem(z_ref[0] + distance, 8)], proj_ref[...], preferred_element_type=F32
            )
            resid = jnp.concatenate([resid_refs[2 * n][...], resid_refs[2 * n + 1][...]], axis=0)
            after = (resid.astype(F32) + mixed).astype(BF16)
            if with_after:
                after_ref[...] = after
            wide = after.astype(F32)
            scale = lax.rsqrt(jnp.mean(wide * wide, axis=1, keepdims=True) + 1e-05)
            normed_ref[2 * half * n : 2 * half * (n + 1)] = (wide * scale * gain_ref[...]).astype(BF16)

    contract = (((1,), (1,)), ((), ()))
    gate = lax.dot_general(normed_ref[...], gate_ref[...], contract, preferred_element_type=F32)
    upward = lax.dot_general(normed_ref[...], up_ref[...], contract, preferred_element_type=F32)
    hidden = (gate / (1.0 + jnp.exp(-gate)) * upward).astype(BF16)
    term = jnp.dot(hidden, down_ref[...], preferred_element_type=F32)

    @pl.when(step == 0)
    def _():
        total_ref[...] = term

    @pl.when(jnp.logical_and(step > 0, step < pl.num_programs(0) - 1))
    def _():
        total_ref[...] += term

    @pl.when(step == pl.num_programs(0) - 1)
    def _():
        final = (total_ref[...] + term).astype(BF16)
        for n in range(2 * count):
            out_refs[n][...] = final[half * n : half * (n + 1)]


def mlp_part(distances, z_index, resid_halves, att_all, out_proj, gain, weights, with_after=False):
    half, width = resid_halves[0].shape
    hidden_rows = weights.shape[0] // 3
    tile = hidden_rows // 2
    rows = 2 * half * len(distances)
    whole = lambda shape: pl.BlockSpec(shape, lambda g, z: (0,) * len(shape))
    weight_spec = lambda kind: pl.BlockSpec((tile, width), lambda g, z: (2 * kind + g % 2, g // 2))
    piece = jax.ShapeDtypeStruct((half, width), BF16)
    out_shape = [piece] * (2 * len(distances))
    out_specs = [whole((half, width))] * (2 * len(distances))
    if with_after:
        out_shape = out_shape + [jax.ShapeDtypeStruct((2 * half, width), BF16)]
        out_specs = out_specs + [whole((2 * half, width))]
    return pl.pallas_call(
        functools.partial(mlp_kernel, distances, with_after),
        out_shape=out_shape,
        grid_spec=pltpu.PrefetchScalarGridSpec(
            num_scalar_prefetch=1,
            grid=(4,),
            in_specs=[whole((half, width))] * (2 * len(distances))
            + [whole(att_all.shape), whole(out_proj.shape), whole(gain.shape)]
            + [weight_spec(0), weight_spec(1), weight_spec(2)],
            out_specs=out_specs,
            scratch_shapes=[pltpu.VMEM((rows, width), BF16), pltpu.VMEM((rows, width), F32)],
        ),
        compiler_params=pltpu.CompilerParams(vmem_limit_bytes=32 * 1024 * 1024),
        cost_estimate=pl.CostEstimate(
            flops=2 * rows * width * 3 * 2 * hidden_rows,
            bytes_accessed=weights.size * 2 + rows * width * 4,
            transcendentals=rows * 2 * hidden_rows,
        ),
        name=f"mlp_{len(distances)}_{distances[0]}",
    )(z_index, *resid_halves, att_all, out_proj, gain, weights, weights, weights)


def per_device(resid, queries, keyvals, piece_order, out_proj, mlp_gain, w_gate, w_up, w_down):
    rows, width = resid.shape
    half = rows // 2
    outer, inner = lax.axis_index("outer"), lax.axis_index("inner")
    core = inner % 2
    z_index = (outer // 2).reshape(1).astype(jnp.int32)

    shard = jnp.concatenate([w_gate.T, w_up.T, w_down], axis=0)
    planes = [[z * 32 + member for member in range(32)] for z in range(8)]
    weights = lax.all_gather(shard, AXES, axis_index_groups=planes, axis=1, tiled=True)

    before = from_previous_block(keyvals)
    both = jnp.concatenate([keyvals, before], axis=1)
    same_core = [[2 * chip + c for chip in range(8)] for c in range(2)]
    own_kv = lax.all_to_all(
        jnp.broadcast_to(both[None], (8,) + both.shape),
        "inner", 0, 0, axis_index_groups=same_core, tiled=True,
    )
    sib_kv = other_core(own_kv)

    a, b = resid[:half], resid[half:]
    part_a, part_b = {0: a}, {0: b}
    right_a = left_a = a
    right_b = left_b = b
    for step in range(1, 5):
        right_a = z_step(right_a, 1)
        left_b = z_step(left_b, -1)
        part_a[8 - step] = right_a
        part_b[step] = left_b
        if step < 4:
            left_a = z_step(left_a, -1)
            right_b = z_step(right_b, 1)
            part_a[step] = left_a
            part_b[8 - step] = right_b

    block_pos = (
        piece_order[:, None] * SPAN + jnp.arange(SPAN, dtype=jnp.int32)[None, :]
    ).reshape(8, 2, rows)
    own_pos = lax.dynamic_index_in_dim(block_pos, core, 1, keepdims=False).reshape(1, 8 * rows)
    sib_pos = lax.dynamic_index_in_dim(block_pos, 1 - core, 1, keepdims=False).reshape(1, 8 * rows)
    query_pos = lax.dynamic_index_in_dim(block_pos.reshape(16, rows), inner, 0, keepdims=False)
    has_before = (outer > 0).astype(jnp.int32).reshape(1)
    attended = pl.pallas_call(
        attention_kernel,
        out_shape=jax.ShapeDtypeStruct((8, rows, QHEADS * HD), BF16),
        in_specs=[pl.BlockSpec(memory_space=pltpu.SMEM)]
        + [pl.BlockSpec(memory_space=pltpu.VMEM)] * 5,
        out_specs=pl.BlockSpec(memory_space=pltpu.VMEM),
        compiler_params=pltpu.CompilerParams(vmem_limit_bytes=40 * 1024 * 1024),
        cost_estimate=pl.CostEstimate(
            flops=4 * 2 * rows * 32 * rows * HD, bytes_accessed=3 * 2**20, transcendentals=2 * rows * 32 * rows
        ),
        name="attention",
    )(has_before, queries, own_kv, sib_kv, query_pos[:, None], jnp.concatenate([own_pos, sib_pos], 0))
    z_groups = [[z * 2 + x_hi for z in range(8)] for x_hi in range(2)]
    att_all = lax.all_to_all(attended, "outer", 0, 0, axis_index_groups=z_groups, tiled=True)

    gain = mlp_gain.reshape(1, width)

    def partial_sums(*distances, with_after=False):
        halves = [h for d in distances for h in (part_a[d], part_b[d])]
        return mlp_part(distances, z_index, halves, att_all, out_proj, gain, weights, with_after)

    sum_a, sum_b = {}, {}
    sum_a[4], sum_b[4] = partial_sums(4)
    for near in (3, 2, 1):
        sum_a[near], sum_b[near], sum_a[8 - near], sum_b[8 - near] = partial_sums(near, 8 - near)
    own_a, own_b, after = partial_sums(0, with_after=True)

    plus = lambda u, v: (u.astype(F32) + v.astype(F32)).astype(BF16)
    right_a, left_b = z_step(sum_a[4], 1), z_step(sum_b[4], -1)
    right_b, left_a = sum_b[3], sum_a[5]
    right_a, left_b = plus(right_a, sum_a[3]), plus(left_b, sum_b[5])
    for near in (2, 1):
        right_a, right_b = z_step(right_a, 1), z_step(right_b, 1)
        left_a, left_b = z_step(left_a, -1), z_step(left_b, -1)
        right_a, right_b = plus(right_a, sum_a[near]), plus(right_b, sum_b[near])
        left_a, left_b = plus(left_a, sum_a[8 - near]), plus(left_b, sum_b[8 - near])
    right_a, right_b = z_step(right_a, 1), z_step(right_b, 1)
    left_a, left_b = z_step(left_a, -1), z_step(left_b, -1)
    wide = lambda v: v.astype(F32)
    mlp_sum = jnp.concatenate(
        [wide(own_a) + wide(right_a) + wide(left_a), wide(own_b) + wide(right_b) + wide(left_b)], axis=0
    )
    return (wide(after) + mlp_sum).astype(BF16)


def solution(mesh):
    placed = (
        P(AXES, None),
        P(AXES, None),
        P(AXES, None),
        P(),
        P(),
        P(),
        P("inner", "outer"),
        P("inner", "outer"),
        P("outer", "inner"),
    )
    return jax.shard_map(
        per_device,
        mesh=mesh,
        in_specs=placed,
        out_specs=P(AXES, None),
        check_vma=False,
    )
```

```python
import functools

import jax
import jax.numpy as jnp
from jax import lax
from jax.experimental import pallas as pl
from jax.experimental.pallas import tpu as pltpu
from jax.sharding import PartitionSpec as P

HD = 128
QHEADS = 2
SPAN = 64
AXES = ("outer", "inner")
F32 = jnp.float32
BF16 = jnp.bfloat16


def device_at(z, x, y, core):
    return ((z * 2 + x // 2) * 2 + x % 2) * 8 + y * 2 + core


def places():
    return [(z, x, y, core) for z in range(8) for x in range(4) for y in range(4) for core in range(2)]


def send(array, target):
    return lax.ppermute(array, AXES, [(device_at(*p), device_at(*target(*p))) for p in places()])


def z_step(array, distance):
    return send(array, lambda z, x, y, core: ((z + distance) % 8, x, y, core))


def from_y(array, distance):
    return send(array, lambda z, x, y, core: (z, x, (y - distance) % 4, core))


def other_core(array):
    return send(array, lambda z, x, y, core: (z, x, y, 1 - core))


def from_block(array, back, other_x):
    def target(z, x, y, core):
        block = (z * 2 + x // 2 + back) % 16
        return (block // 2, block % 2 * 2 + (x % 2 ^ other_x), y, core)

    return send(array, target)


def attention_kernel(place_ref, order_ref, q_ref, *refs):
    kv_refs, out_ref = refs[:-1], refs[-1]
    rows = q_ref.shape[0]
    outer, inner = place_ref[0], place_ref[1]
    x_lo, y, core = inner // 8, lax.rem(inner // 2, 4), lax.rem(inner, 2)
    q = jnp.concatenate([q_ref[:, :HD], q_ref[:, HD:]], axis=0)

    def positions(member, dim):
        shape = (1, rows) if dim else (rows, 1)
        r = lax.broadcasted_iota(jnp.int32, shape, dim)
        return jnp.where(
            r < SPAN, order_ref[2 * member] * SPAN + r, order_ref[2 * member + 1] * SPAN + r - SPAN
        )

    qpos = positions(inner, 0)
    qpos = jnp.concatenate([qpos, qpos], axis=0)
    kpos, own, before = [], [], []
    for from_core in range(2):
        for step in range(4):
            block = kv_refs[4 * from_core + step]
            for other_x in range(2):
                member = (
                    lax.rem(x_lo + other_x, 2) * 8 + lax.rem(y + step, 4) * 2 + lax.rem(core + from_core, 2)
                )
                kpos.append(positions(member, 1))
                own.append(block[:, 4 * HD * other_x : 4 * HD * other_x + 2 * HD])
                before.append(block[:, 4 * HD * other_x + 2 * HD : 4 * HD * (other_x + 1)])
    kpos = jnp.concatenate(kpos, axis=1)
    own, before = jnp.concatenate(own, axis=0), jnp.concatenate(before, axis=0)
    contract = (((1,), (1,)), ((), ()))
    scale = HD ** (-0.5)
    own_score = lax.dot_general(q, own[:, :HD], contract, preferred_element_type=F32) * scale
    before_score = lax.dot_general(q, before[:, :HD], contract, preferred_element_type=F32) * scale
    own_seen = kpos <= qpos
    before_seen = jnp.broadcast_to(outer > 0, before_score.shape)
    own_score = jnp.where(own_seen, own_score, -1e30)
    before_score = jnp.where(before_seen, before_score, -1e30)
    top = jnp.maximum(
        jnp.max(own_score, axis=1, keepdims=True), jnp.max(before_score, axis=1, keepdims=True)
    )
    own_weight = jnp.where(own_seen, jnp.exp(own_score - top), 0.0)
    before_weight = jnp.where(before_seen, jnp.exp(before_score - top), 0.0)
    total = jnp.sum(own_weight, axis=1, keepdims=True) + jnp.sum(before_weight, axis=1, keepdims=True)
    mixed = jnp.dot(own_weight.astype(BF16), own[:, HD:], preferred_element_type=F32)
    mixed = mixed + jnp.dot(before_weight.astype(BF16), before[:, HD:], preferred_element_type=F32)
    attended = (mixed / total).astype(BF16)
    attended = jnp.concatenate([attended[:rows], attended[rows:]], axis=1)
    for copy in range(out_ref.shape[0]):
        out_ref[copy] = attended


def mlp_kernel(distances, resid_counts, with_after, place_ref, att_ref, proj_ref, gain_ref, weight_ref, *refs):
    inputs = sum(resid_counts)
    resid_refs, refs = refs[:inputs], refs[inputs:]
    out_refs = refs[: 2 * len(distances)]
    z = place_ref[0] // 2
    normed, first = [], 0
    for distance, pieces in zip(distances, resid_counts):
        resid = jnp.concatenate([r[...] for r in resid_refs[first : first + pieces]], axis=0)
        first += pieces
        mixed = jnp.dot(
            att_ref[lax.rem(z + distance, 8)], proj_ref[...], preferred_element_type=F32
        )
        after = (resid.astype(F32) + mixed).astype(BF16)
        if with_after:
            refs[-1][...] = after
        wide = after.astype(F32)
        scale = lax.rsqrt(jnp.mean(wide * wide, axis=1, keepdims=True) + 1e-05)
        normed.append((wide * scale * gain_ref[...]).astype(BF16))
    normed = jnp.concatenate(normed, axis=0)
    total = None
    units = weight_ref.shape[1] // 3
    wide_units = units // HD * HD
    for x_hi in range(2):
        members = slice(16 * x_hi, 16 * x_hi + 16)
        columns = [
            weight_ref[members, HD * tile : HD * (tile + 1), :].reshape(16 * HD, HD)
            for tile in range(2 * units // HD)
        ]
        both = jnp.dot(normed, jnp.concatenate(columns, axis=1), preferred_element_type=F32)
        gate, upward, last = (
            both[:, :wide_units],
            both[:, wide_units : 2 * wide_units],
            both[:, 2 * wide_units :],
        )
        silu = lambda v: v / (1.0 + jnp.exp(-v))
        last = silu(last) * pltpu.roll(last, HD // 2, 1)
        hidden = jnp.concatenate([silu(gate) * upward, last[:, : HD // 2]], axis=1).astype(BF16)
        down = jnp.concatenate(
            [weight_ref[16 * x_hi + m, 2 * units :, :] for m in range(16)], axis=1
        )
        term = jnp.dot(hidden, down, preferred_element_type=F32)
        total = term if total is None else total + term
    final = total.astype(BF16)
    half = out_refs[0].shape[0]
    for n, ref in enumerate(out_refs):
        ref[...] = final[half * n : half * (n + 1)]


def mlp_part(distances, place, resid_pieces, att_all, out_proj, gain, weights, with_after=False):
    width = gain.shape[1]
    rows = att_all.shape[1]
    piece = jax.ShapeDtypeStruct((rows // 2, width), BF16)
    out_shape = [piece] * (2 * len(distances))
    if with_after:
        out_shape = out_shape + [jax.ShapeDtypeStruct((rows, width), BF16)]
    vmem = pl.BlockSpec(memory_space=pltpu.VMEM)
    pieces = [p for some in resid_pieces for p in some]
    count = rows * len(distances)
    return pl.pallas_call(
        functools.partial(mlp_kernel, distances, [len(some) for some in resid_pieces], with_after),
        out_shape=out_shape,
        in_specs=[pl.BlockSpec(memory_space=pltpu.SMEM)] + [vmem] * (4 + len(pieces)),
        out_specs=[vmem] * len(out_shape),
        compiler_params=pltpu.CompilerParams(vmem_limit_bytes=32 * 1024 * 1024),
        cost_estimate=pl.CostEstimate(
            flops=2 * count * weights.size, bytes_accessed=weights.size * 2, transcendentals=count * 1024
        ),
        name=f"mlp_{len(distances)}_{distances[0]}",
    )(place, att_all, out_proj, gain, weights, *pieces)


def per_device(resid, queries, keyvals, piece_order, out_proj, mlp_gain, w_gate, w_up, w_down):
    rows, width = resid.shape
    half = rows // 2
    units = w_down.shape[0]
    wide_units = units // HD * HD
    place = jnp.stack([lax.axis_index("outer"), lax.axis_index("inner")]).astype(jnp.int32)

    gate_up = jnp.concatenate(
        [w_gate[:, :wide_units], w_up[:, :wide_units], w_gate[:, wide_units:], w_up[:, wide_units:]], axis=1
    )
    gate_up = gate_up.reshape(HD, 2 * units // HD, HD).transpose(1, 0, 2).reshape(2 * units, HD)
    shard = jnp.concatenate([gate_up, w_down], axis=0)
    planes = [[z * 32 + member for member in range(32)] for z in range(8)]
    weights = lax.all_gather(shard, AXES, axis_index_groups=planes, axis=0)
    weights = pltpu.with_memory_space_constraint(weights, pltpu.VMEM)

    across_x = jnp.concatenate(
        [keyvals, from_block(keyvals, 1, 0), from_block(keyvals, 0, 1), from_block(keyvals, 1, 1)], axis=1
    )
    pieces = {0: [resid]}
    right, left = z_step(resid, 1), z_step(resid, -1)
    across_x, right, left = lax.optimization_barrier((across_x, right, left))
    pieces[7], pieces[1] = [right], [left]
    own_kv = [across_x] + [from_y(across_x, step) for step in (1, 2, 3)]
    right, left = z_step(right, 1), z_step(left, -1)
    far = jnp.concatenate(own_kv[1:], axis=0)
    far, right, left = lax.optimization_barrier((far, right, left))
    pieces[6], pieces[2] = [right], [left]
    far = other_core(far)
    sib_kv = [other_core(across_x)] + [far[rows * n : rows * (n + 1)] for n in range(3)]
    attended = pl.pallas_call(
        attention_kernel,
        out_shape=jax.ShapeDtypeStruct((8, rows, QHEADS * HD), BF16),
        in_specs=[pl.BlockSpec(memory_space=pltpu.SMEM)] * 2
        + [pl.BlockSpec(memory_space=pltpu.VMEM)] * 9,
        out_specs=pl.BlockSpec(memory_space=pltpu.VMEM),
        compiler_params=pltpu.CompilerParams(vmem_limit_bytes=32 * 1024 * 1024),
        cost_estimate=pl.CostEstimate(
            flops=4 * 2 * rows * 32 * rows * HD, bytes_accessed=3 * 2**20, transcendentals=2 * rows * 32 * rows
        ),
        name="attention",
    )(place, piece_order, queries, *own_kv, *sib_kv)
    right, left = z_step(right, 1), z_step(left, -1)
    attended, right, left = lax.optimization_barrier((attended, right, left))
    pieces[5], pieces[3] = [right], [left]
    pieces[4] = [z_step(right[:half], 1), z_step(left[half:], -1)]
    z_groups = [[z * 2 + x_hi for z in range(8)] for x_hi in range(2)]
    att_all = lax.all_to_all(attended, "outer", 0, 0, axis_index_groups=z_groups, tiled=True)

    gain = mlp_gain.reshape(1, width)

    def partial_sums(after, *distances, with_after=False):
        ready = lax.optimization_barrier((att_all,) + after)[0]
        return mlp_part(
            distances, place, [pieces[d] for d in distances], ready, out_proj, gain, weights, with_after
        )

    plus = lambda u, v: (u.astype(F32) + v.astype(F32)).astype(BF16)
    far_a, far_b = partial_sums((), 4)
    right_a, left_b = z_step(far_a, 1), z_step(far_b, -1)
    sums = partial_sums((far_a,), 3, 5)
    right_b, left_a = z_step(sums[1], 1), z_step(sums[2], -1)
    right_a, left_b = plus(right_a, sums[0]), plus(left_b, sums[3])
    for near in (2, 1):
        sums = partial_sums((right_a, left_b), near, 8 - near)
        right_a, left_b = z_step(right_a, 1), z_step(left_b, -1)
        right_b, left_a = plus(right_b, sums[1]), plus(left_a, sums[2])
        right_b, left_a = z_step(right_b, 1), z_step(left_a, -1)
        right_a, left_b = plus(right_a, sums[0]), plus(left_b, sums[3])
    own_a, own_b, after = partial_sums((right_a, left_b), 0, with_after=True)
    right_a, left_b = z_step(right_a, 1), z_step(left_b, -1)
    wide = lambda v: v.astype(F32)
    mlp_sum = jnp.concatenate(
        [wide(own_a) + wide(right_a) + wide(left_a), wide(own_b) + wide(right_b) + wide(left_b)], axis=0
    )
    return (wide(after) + mlp_sum).astype(BF16)


def solution(mesh):
    placed = (
        P(AXES, None),
        P(AXES, None),
        P(AXES, None),
        P(),
        P(),
        P(),
        P("inner", "outer"),
        P("inner", "outer"),
        P("outer", "inner"),
    )
    return jax.shard_map(
        per_device,
        mesh=mesh,
        in_specs=placed,
        out_specs=P(AXES, None),
        check_vma=False,
    )
```

```python
import functools

import jax
import jax.numpy as jnp
from jax import lax
from jax.experimental import pallas as pl
from jax.experimental.pallas import tpu as pltpu
from jax.sharding import PartitionSpec as P

HD = 128
QHEADS = 2
SPAN = 64
AXES = ("outer", "inner")
F32 = jnp.float32
BF16 = jnp.bfloat16


def device_at(z, x, y, core):
    return ((z * 2 + x // 2) * 2 + x % 2) * 8 + y * 2 + core


def places():
    return [(z, x, y, core) for z in range(8) for x in range(4) for y in range(4) for core in range(2)]


def send(array, target):
    return lax.ppermute(array, AXES, [(device_at(*p), device_at(*target(*p))) for p in places()])


def z_step(array, distance):
    return send(array, lambda z, x, y, core: ((z + distance) % 8, x, y, core))


def from_y(array, distance):
    return send(array, lambda z, x, y, core: (z, x, (y - distance) % 4, core))


def other_core(array):
    return send(array, lambda z, x, y, core: (z, x, y, 1 - core))


def from_block(array, back, other_x):
    def target(z, x, y, core):
        block = (z * 2 + x // 2 + back) % 16
        return (block // 2, block % 2 * 2 + (x % 2 ^ other_x), y, core)

    return send(array, target)


def attention_kernel(place_ref, order_ref, q_ref, *refs):
    kv_refs, out_ref = refs[:-1], refs[-1]
    rows = q_ref.shape[0]
    outer, inner = place_ref[0], place_ref[1]
    x_lo, y, core = inner // 8, lax.rem(inner // 2, 4), lax.rem(inner, 2)
    q = jnp.concatenate([q_ref[:, :HD], q_ref[:, HD:]], axis=0)

    def positions(member, dim):
        shape = (1, rows) if dim else (rows, 1)
        r = lax.broadcasted_iota(jnp.int32, shape, dim)
        return jnp.where(
            r < SPAN, order_ref[2 * member] * SPAN + r, order_ref[2 * member + 1] * SPAN + r - SPAN
        )

    qpos = positions(inner, 0)
    qpos = jnp.concatenate([qpos, qpos], axis=0)
    kpos, own, before = [], [], []
    for from_core in range(2):
        for step in range(4):
            block = kv_refs[4 * from_core + step]
            for other_x in range(2):
                member = (
                    lax.rem(x_lo + other_x, 2) * 8 + lax.rem(y + step, 4) * 2 + lax.rem(core + from_core, 2)
                )
                kpos.append(positions(member, 1))
                own.append(block[:, 4 * HD * other_x : 4 * HD * other_x + 2 * HD])
                before.append(block[:, 4 * HD * other_x + 2 * HD : 4 * HD * (other_x + 1)])
    kpos = jnp.concatenate(kpos, axis=1)
    own, before = jnp.concatenate(own, axis=0), jnp.concatenate(before, axis=0)
    contract = (((1,), (1,)), ((), ()))
    scale = HD ** (-0.5)
    own_score = lax.dot_general(q, own[:, :HD], contract, preferred_element_type=F32) * scale
    before_score = lax.dot_general(q, before[:, :HD], contract, preferred_element_type=F32) * scale
    own_seen = kpos <= qpos
    before_seen = jnp.broadcast_to(outer > 0, before_score.shape)
    own_score = jnp.where(own_seen, own_score, -1e30)
    before_score = jnp.where(before_seen, before_score, -1e30)
    top = jnp.maximum(
        jnp.max(own_score, axis=1, keepdims=True), jnp.max(before_score, axis=1, keepdims=True)
    )
    own_weight = jnp.where(own_seen, jnp.exp(own_score - top), 0.0)
    before_weight = jnp.where(before_seen, jnp.exp(before_score - top), 0.0)
    total = jnp.sum(own_weight, axis=1, keepdims=True) + jnp.sum(before_weight, axis=1, keepdims=True)
    mixed = jnp.dot(own_weight.astype(BF16), own[:, HD:], preferred_element_type=F32)
    mixed = mixed + jnp.dot(before_weight.astype(BF16), before[:, HD:], preferred_element_type=F32)
    attended = (mixed / total).astype(BF16)
    attended = jnp.concatenate([attended[:rows], attended[rows:]], axis=1)
    for copy in range(out_ref.shape[0]):
        out_ref[copy] = attended


def shard_kernel(gate_ref, up_ref, down_ref, out_ref):
    wide = gate_ref.shape[0] // HD
    tiles = [ref[HD * t : HD * (t + 1)] for ref in (gate_ref, up_ref) for t in range(wide)]
    tiles.append(jnp.concatenate([gate_ref[HD * wide :], up_ref[HD * wide :]], axis=0))
    for t, tile in enumerate(tiles):
        out_ref[HD * t : HD * (t + 1)] = tile.astype(F32).T.astype(BF16)
    out_ref[HD * len(tiles) :] = down_ref[...]


def mlp_kernel(distances, resid_counts, with_after, place_ref, att_ref, proj_ref, gain_ref, weight_ref, *refs):
    inputs = sum(resid_counts)
    resid_refs, refs = refs[:inputs], refs[inputs:]
    out_refs = refs[: 2 * len(distances)]
    z = place_ref[0] // 2
    normed, first = [], 0
    for distance, pieces in zip(distances, resid_counts):
        resid = jnp.concatenate([r[...] for r in resid_refs[first : first + pieces]], axis=0)
        first += pieces
        mixed = jnp.dot(
            att_ref[lax.rem(z + distance, 8)], proj_ref[...], preferred_element_type=F32
        )
        after = (resid.astype(F32) + mixed).astype(BF16)
        if with_after:
            refs[-1][...] = after
        wide = after.astype(F32)
        scale = lax.rsqrt(jnp.mean(wide * wide, axis=1, keepdims=True) + 1e-05)
        normed.append((wide * scale * gain_ref[...]).astype(BF16))
    normed = jnp.concatenate(normed, axis=0)
    total = None
    units = weight_ref.shape[1] // 3
    wide_units = units // HD * HD
    for x_hi in range(2):
        members = slice(16 * x_hi, 16 * x_hi + 16)
        columns = [
            weight_ref[members, HD * tile : HD * (tile + 1), :].reshape(16 * HD, HD)
            for tile in range(2 * units // HD)
        ]
        both = jnp.dot(normed, jnp.concatenate(columns, axis=1), preferred_element_type=F32)
        gate, upward, last = (
            both[:, :wide_units],
            both[:, wide_units : 2 * wide_units],
            both[:, 2 * wide_units :],
        )
        silu = lambda v: v / (1.0 + jnp.exp(-v))
        last = silu(last) * pltpu.roll(last, HD // 2, 1)
        hidden = jnp.concatenate([silu(gate) * upward, last[:, : HD // 2]], axis=1).astype(BF16)
        down = jnp.concatenate(
            [weight_ref[16 * x_hi + m, 2 * units :, :] for m in range(16)], axis=1
        )
        term = jnp.dot(hidden, down, preferred_element_type=F32)
        total = term if total is None else total + term
    final = total.astype(BF16)
    half = out_refs[0].shape[0]
    for n, ref in enumerate(out_refs):
        ref[...] = final[half * n : half * (n + 1)]


def mlp_part(distances, place, resid_pieces, att_all, out_proj, gain, weights, with_after=False):
    width = gain.shape[1]
    rows = att_all.shape[1]
    piece = jax.ShapeDtypeStruct((rows // 2, width), BF16)
    out_shape = [piece] * (2 * len(distances))
    if with_after:
        out_shape = out_shape + [jax.ShapeDtypeStruct((rows, width), BF16)]
    vmem = pl.BlockSpec(memory_space=pltpu.VMEM)
    pieces = [p for some in resid_pieces for p in some]
    count = rows * len(distances)
    return pl.pallas_call(
        functools.partial(mlp_kernel, distances, [len(some) for some in resid_pieces], with_after),
        out_shape=out_shape,
        in_specs=[pl.BlockSpec(memory_space=pltpu.SMEM)] + [vmem] * (4 + len(pieces)),
        out_specs=[vmem] * len(out_shape),
        compiler_params=pltpu.CompilerParams(vmem_limit_bytes=32 * 1024 * 1024),
        cost_estimate=pl.CostEstimate(
            flops=2 * count * weights.size, bytes_accessed=weights.size * 2, transcendentals=count * 1024
        ),
        name=f"mlp_{len(distances)}_{distances[0]}",
    )(place, att_all, out_proj, gain, weights, *pieces)


def per_device(resid, queries, keyvals, piece_order, out_proj, mlp_gain, w_gate, w_up, w_down):
    rows, width = resid.shape
    half = rows // 2
    place = jnp.stack([lax.axis_index("outer"), lax.axis_index("inner")]).astype(jnp.int32)

    shard = pl.pallas_call(
        shard_kernel,
        out_shape=jax.ShapeDtypeStruct((3 * w_down.shape[0], HD), BF16),
        in_specs=[pl.BlockSpec(memory_space=pltpu.VMEM)] * 3,
        out_specs=pl.BlockSpec(memory_space=pltpu.VMEM),
        name="shard",
    )(w_gate.T, w_up.T, w_down)
    planes = [[z * 32 + member for member in range(32)] for z in range(8)]
    weights = lax.all_gather(shard, AXES, axis_index_groups=planes, axis=0)
    weights = pltpu.with_memory_space_constraint(weights, pltpu.VMEM)

    across_x = jnp.concatenate(
        [keyvals, from_block(keyvals, 1, 0), from_block(keyvals, 0, 1), from_block(keyvals, 1, 1)], axis=1
    )
    pieces = {0: [resid]}
    right, left = z_step(resid, 1), z_step(resid, -1)
    across_x, right, left = lax.optimization_barrier((across_x, right, left))
    pieces[7], pieces[1] = [right], [left]
    own_kv = [across_x] + [from_y(across_x, step) for step in (1, 2, 3)]
    right, left = z_step(right, 1), z_step(left, -1)
    far = jnp.concatenate(own_kv[1:], axis=0)
    far, right, left = lax.optimization_barrier((far, right, left))
    pieces[6], pieces[2] = [right], [left]
    far = other_core(far)
    sib_kv = [other_core(across_x)] + [far[rows * n : rows * (n + 1)] for n in range(3)]
    attended = pl.pallas_call(
        attention_kernel,
        out_shape=jax.ShapeDtypeStruct((8, rows, QHEADS * HD), BF16),
        in_specs=[pl.BlockSpec(memory_space=pltpu.SMEM)] * 2
        + [pl.BlockSpec(memory_space=pltpu.VMEM)] * 9,
        out_specs=pl.BlockSpec(memory_space=pltpu.VMEM),
        compiler_params=pltpu.CompilerParams(vmem_limit_bytes=32 * 1024 * 1024),
        cost_estimate=pl.CostEstimate(
            flops=4 * 2 * rows * 32 * rows * HD, bytes_accessed=3 * 2**20, transcendentals=2 * rows * 32 * rows
        ),
        name="attention",
    )(place, piece_order, queries, *own_kv, *sib_kv)
    right_a, left_b = z_step(right[:half], 1), z_step(left[half:], -1)
    attended, right_a, left_b = lax.optimization_barrier((attended, right_a, left_b))
    pieces[5] = [right_a, z_step(right[half:], 1)]
    pieces[3] = [z_step(left[:half], -1), left_b]
    pieces[4] = [z_step(right_a, 1), z_step(left_b, -1)]
    z_groups = [[z * 2 + x_hi for z in range(8)] for x_hi in range(2)]
    att_all = lax.all_to_all(attended, "outer", 0, 0, axis_index_groups=z_groups, tiled=True)

    gain = mlp_gain.reshape(1, width)

    def partial_sums(after, *distances, with_after=False):
        ready = lax.optimization_barrier((att_all,) + after)[0]
        return mlp_part(
            distances, place, [pieces[d] for d in distances], ready, out_proj, gain, weights, with_after
        )

    plus = lambda u, v: (u.astype(F32) + v.astype(F32)).astype(BF16)
    far_a, far_b = partial_sums((), 4)
    right_a, left_b = z_step(far_a, 1), z_step(far_b, -1)
    sums = partial_sums((far_a,), 3, 5)
    right_b, left_a = z_step(sums[1], 1), z_step(sums[2], -1)
    right_a, left_b = plus(right_a, sums[0]), plus(left_b, sums[3])
    for near in (2, 1):
        sums = partial_sums((right_a, left_b), near, 8 - near)
        right_a, left_b = z_step(right_a, 1), z_step(left_b, -1)
        right_b, left_a = plus(right_b, sums[1]), plus(left_a, sums[2])
        right_b, left_a = z_step(right_b, 1), z_step(left_a, -1)
        right_a, left_b = plus(right_a, sums[0]), plus(left_b, sums[3])
    own_a, own_b, after = partial_sums((right_a, left_b), 0, with_after=True)
    right_a, left_b = z_step(right_a, 1), z_step(left_b, -1)
    wide = lambda v: v.astype(F32)
    mlp_sum = jnp.concatenate(
        [wide(own_a) + wide(right_a) + wide(left_a), wide(own_b) + wide(right_b) + wide(left_b)], axis=0
    )
    return (wide(after) + mlp_sum).astype(BF16)


def solution(mesh):
    placed = (
        P(AXES, None),
        P(AXES, None),
        P(AXES, None),
        P(),
        P(),
        P(),
        P("inner", "outer"),
        P("inner", "outer"),
        P("outer", "inner"),
    )
    return jax.shard_map(
        per_device,
        mesh=mesh,
        in_specs=placed,
        out_specs=P(AXES, None),
        check_vma=False,
    )
```

```python
import functools

import jax
import jax.numpy as jnp
from jax import lax
from jax.experimental import pallas as pl
from jax.experimental.pallas import tpu as pltpu
from jax.sharding import PartitionSpec as P

HD = 128
QHEADS = 2
SPAN = 64
AXES = ("outer", "inner")
F32 = jnp.float32
BF16 = jnp.bfloat16


def device_at(z, x, y, core):
    return ((z * 2 + x // 2) * 2 + x % 2) * 8 + y * 2 + core


def places():
    return [(z, x, y, core) for z in range(8) for x in range(4) for y in range(4) for core in range(2)]


def send(array, target):
    return lax.ppermute(array, AXES, [(device_at(*p), device_at(*target(*p))) for p in places()])


def z_step(array, distance):
    return send(array, lambda z, x, y, core: ((z + distance) % 8, x, y, core))


def from_y(array, distance):
    return send(array, lambda z, x, y, core: (z, x, (y - distance) % 4, core))


def other_core(array):
    return send(array, lambda z, x, y, core: (z, x, y, 1 - core))


def from_block(array, back, other_x):
    def target(z, x, y, core):
        block = (z * 2 + x // 2 + back) % 16
        return (block // 2, block % 2 * 2 + (x % 2 ^ other_x), y, core)

    return send(array, target)


def attention_kernel(place_ref, order_ref, q_ref, *refs):
    kv_refs, out_ref = refs[:-1], refs[-1]
    rows = q_ref.shape[0]
    outer, inner = place_ref[0], place_ref[1]
    x_lo, y, core = inner // 8, lax.rem(inner // 2, 4), lax.rem(inner, 2)
    q = jnp.concatenate([q_ref[:, :HD], q_ref[:, HD:]], axis=0)

    def positions(member, dim):
        shape = (1, rows) if dim else (rows, 1)
        r = lax.broadcasted_iota(jnp.int32, shape, dim)
        return jnp.where(
            r < SPAN, order_ref[2 * member] * SPAN + r, order_ref[2 * member + 1] * SPAN + r - SPAN
        )

    qpos = positions(inner, 0)
    qpos = jnp.concatenate([qpos, qpos], axis=0)
    kpos, own, before = [], [], []
    for from_core in range(2):
        for step in range(4):
            block = kv_refs[4 * from_core + step]
            for other_x in range(2):
                member = (
                    lax.rem(x_lo + other_x, 2) * 8 + lax.rem(y + step, 4) * 2 + lax.rem(core + from_core, 2)
                )
                kpos.append(positions(member, 1))
                own.append(block[:, 4 * HD * other_x : 4 * HD * other_x + 2 * HD])
                before.append(block[:, 4 * HD * other_x + 2 * HD : 4 * HD * (other_x + 1)])
    kpos = jnp.concatenate(kpos, axis=1)
    own, before = jnp.concatenate(own, axis=0), jnp.concatenate(before, axis=0)
    contract = (((1,), (1,)), ((), ()))
    scale = HD ** (-0.5)
    own_score = lax.dot_general(q, own[:, :HD], contract, preferred_element_type=F32) * scale
    before_score = lax.dot_general(q, before[:, :HD], contract, preferred_element_type=F32) * scale
    own_seen = kpos <= qpos
    before_seen = jnp.broadcast_to(outer > 0, before_score.shape)
    own_score = jnp.where(own_seen, own_score, -1e30)
    before_score = jnp.where(before_seen, before_score, -1e30)
    top = jnp.maximum(
        jnp.max(own_score, axis=1, keepdims=True), jnp.max(before_score, axis=1, keepdims=True)
    )
    own_weight = jnp.where(own_seen, jnp.exp(own_score - top), 0.0)
    before_weight = jnp.where(before_seen, jnp.exp(before_score - top), 0.0)
    total = jnp.sum(own_weight, axis=1, keepdims=True) + jnp.sum(before_weight, axis=1, keepdims=True)
    mixed = jnp.dot(own_weight.astype(BF16), own[:, HD:], preferred_element_type=F32)
    mixed = mixed + jnp.dot(before_weight.astype(BF16), before[:, HD:], preferred_element_type=F32)
    attended = (mixed / total).astype(BF16)
    attended = jnp.concatenate([attended[:rows], attended[rows:]], axis=1)
    for copy in range(out_ref.shape[0]):
        out_ref[copy] = attended


def shard_kernel(gate_ref, up_ref, down_ref, out_ref):
    wide = gate_ref.shape[0] // HD
    tiles = [ref[HD * t : HD * (t + 1)] for ref in (gate_ref, up_ref) for t in range(wide)]
    tiles.append(jnp.concatenate([gate_ref[HD * wide :], up_ref[HD * wide :]], axis=0))
    for t, tile in enumerate(tiles):
        out_ref[HD * t : HD * (t + 1)] = tile.astype(F32).T.astype(BF16)
    out_ref[HD * len(tiles) :] = down_ref[...]


def mlp_kernel(
    distances, resid_counts, with_after, loads, place_ref, att_ref, proj_ref, gain_ref, weight_ref, *refs
):
    copies = []
    if loads:
        source, weight_ref, sems = weight_ref, refs[-2], refs[-1]
        split = weight_ref.shape[1] // 3 * 2
        for n, x_hi in enumerate((0, 1)):
            for k, rows in enumerate((pl.ds(0, split), pl.ds(split, split // 2))):
                part = (pl.ds(16 * x_hi, 16), rows)
                copies.append(pltpu.make_async_copy(source.at[part], weight_ref.at[part], sems.at[2 * n + k]))
        for copy in copies:
            copy.start()
    inputs = sum(resid_counts)
    resid_refs, refs = refs[:inputs], refs[inputs:]
    out_refs = refs[: 2 * len(distances)]
    z = place_ref[0] // 2
    normed, first = [], 0
    for distance, pieces in zip(distances, resid_counts):
        resid = jnp.concatenate([r[...] for r in resid_refs[first : first + pieces]], axis=0)
        first += pieces
        mixed = jnp.dot(
            att_ref[lax.rem(z + distance, 8)], proj_ref[...], preferred_element_type=F32
        )
        after = (resid.astype(F32) + mixed).astype(BF16)
        if with_after:
            refs[-1][...] = after
        wide = after.astype(F32)
        scale = lax.rsqrt(jnp.mean(wide * wide, axis=1, keepdims=True) + 1e-05)
        normed.append((wide * scale * gain_ref[...]).astype(BF16))
    normed = jnp.concatenate(normed, axis=0)
    total = None
    units = weight_ref.shape[1] // 3
    wide_units = units // HD * HD
    for x_hi in range(2):
        members = slice(16 * x_hi, 16 * x_hi + 16)
        if loads:
            copies[2 * x_hi].wait()
        columns = [
            weight_ref[members, HD * tile : HD * (tile + 1), :].reshape(16 * HD, HD)
            for tile in range(2 * units // HD)
        ]
        both = jnp.dot(normed, jnp.concatenate(columns, axis=1), preferred_element_type=F32)
        gate, upward, last = (
            both[:, :wide_units],
            both[:, wide_units : 2 * wide_units],
            both[:, 2 * wide_units :],
        )
        silu = lambda v: v / (1.0 + jnp.exp(-v))
        last = silu(last) * pltpu.roll(last, HD // 2, 1)
        hidden = jnp.concatenate([silu(gate) * upward, last[:, : HD // 2]], axis=1).astype(BF16)
        if loads:
            copies[2 * x_hi + 1].wait()
        down = jnp.concatenate(
            [weight_ref[16 * x_hi + m, 2 * units :, :] for m in range(16)], axis=1
        )
        term = jnp.dot(hidden, down, preferred_element_type=F32)
        total = term if total is None else total + term
    final = total.astype(BF16)
    half = out_refs[0].shape[0]
    for n, ref in enumerate(out_refs):
        ref[...] = final[half * n : half * (n + 1)]


def mlp_part(distances, place, resid_pieces, att_all, out_proj, gain, weights, with_after=False, loads=False):
    width = gain.shape[1]
    rows = att_all.shape[1]
    piece = jax.ShapeDtypeStruct((rows // 2, width), BF16)
    out_shape = [piece] * (2 * len(distances))
    if with_after:
        out_shape = out_shape + [jax.ShapeDtypeStruct((rows, width), BF16)]
    scratch = []
    if loads:
        out_shape = out_shape + [pltpu.VMEM(weights.shape, BF16)]
        scratch = [pltpu.SemaphoreType.DMA((4,))]
    vmem = pl.BlockSpec(memory_space=pltpu.VMEM)
    pieces = [p for some in resid_pieces for p in some]
    count = rows * len(distances)
    return pl.pallas_call(
        functools.partial(mlp_kernel, distances, [len(some) for some in resid_pieces], with_after, loads),
        out_shape=out_shape,
        in_specs=[pl.BlockSpec(memory_space=pltpu.SMEM)]
        + [vmem] * 3
        + [pl.BlockSpec(memory_space=pl.ANY) if loads else vmem]
        + [vmem] * len(pieces),
        out_specs=[vmem] * len(out_shape),
        scratch_shapes=scratch,
        compiler_params=pltpu.CompilerParams(vmem_limit_bytes=32 * 1024 * 1024),
        cost_estimate=pl.CostEstimate(
            flops=2 * count * weights.size, bytes_accessed=weights.size * 2, transcendentals=count * 1024
        ),
        name=f"mlp_{len(distances)}_{distances[0]}",
    )(place, att_all, out_proj, gain, weights, *pieces)


def per_device(resid, queries, keyvals, piece_order, out_proj, mlp_gain, w_gate, w_up, w_down):
    rows, width = resid.shape
    half = rows // 2
    place = jnp.stack([lax.axis_index("outer"), lax.axis_index("inner")]).astype(jnp.int32)

    shard = pl.pallas_call(
        shard_kernel,
        out_shape=jax.ShapeDtypeStruct((3 * w_down.shape[0], HD), BF16),
        in_specs=[pl.BlockSpec(memory_space=pltpu.VMEM)] * 3,
        out_specs=pl.BlockSpec(memory_space=pltpu.VMEM),
        name="shard",
    )(w_gate.T, w_up.T, w_down)
    planes = [[z * 32 + member for member in range(32)] for z in range(8)]
    weights = lax.all_gather(shard, AXES, axis_index_groups=planes, axis=0)

    across_x = jnp.concatenate(
        [keyvals, from_block(keyvals, 1, 0), from_block(keyvals, 0, 1), from_block(keyvals, 1, 1)], axis=1
    )
    pieces = {0: [resid]}
    ring_start = lax.optimization_barrier((resid, across_x))[0]
    right, left = z_step(ring_start, 1), z_step(ring_start, -1)
    pieces[7], pieces[1] = [right], [left]
    own_kv = [across_x] + [from_y(across_x, step) for step in (1, 2, 3)]
    right, left = z_step(right, 1), z_step(left, -1)
    far = jnp.concatenate(own_kv[1:], axis=0)
    far, right, left = lax.optimization_barrier((far, right, left))
    pieces[6], pieces[2] = [right], [left]
    far = other_core(far)
    sib_kv = [other_core(across_x)] + [far[rows * n : rows * (n + 1)] for n in range(3)]
    attended = pl.pallas_call(
        attention_kernel,
        out_shape=jax.ShapeDtypeStruct((8, rows, QHEADS * HD), BF16),
        in_specs=[pl.BlockSpec(memory_space=pltpu.SMEM)] * 2
        + [pl.BlockSpec(memory_space=pltpu.VMEM)] * 9,
        out_specs=pl.BlockSpec(memory_space=pltpu.VMEM),
        compiler_params=pltpu.CompilerParams(vmem_limit_bytes=32 * 1024 * 1024),
        cost_estimate=pl.CostEstimate(
            flops=4 * 2 * rows * 32 * rows * HD, bytes_accessed=3 * 2**20, transcendentals=2 * rows * 32 * rows
        ),
        name="attention",
    )(place, piece_order, queries, *own_kv, *sib_kv)
    right_a, left_b = z_step(right[:half], 1), z_step(left[half:], -1)
    attended, right_a, left_b = lax.optimization_barrier((attended, right_a, left_b))
    pieces[4] = [z_step(right_a, 1), z_step(left_b, -1)]
    z_groups = [[z * 2 + x_hi for z in range(8)] for x_hi in range(2)]
    att_all = lax.all_to_all(attended, "outer", 0, 0, axis_index_groups=z_groups, tiled=True)

    late = lax.optimization_barrier((right[half:], left[:half], att_all))
    pieces[5] = [right_a, z_step(late[0], 1)]
    pieces[3] = [z_step(late[1], -1), left_b]

    gain = mlp_gain.reshape(1, width)

    def partial_sums(after, *distances, with_after=False, loads=False):
        ready = lax.optimization_barrier((att_all,) + after)[0]
        return mlp_part(
            distances, place, [pieces[d] for d in distances], ready, out_proj, gain, weights, with_after, loads
        )

    plus = lambda u, v: (u.astype(F32) + v.astype(F32)).astype(BF16)
    far_a, far_b, weights = partial_sums((), 4, loads=True)
    weights = pltpu.with_memory_space_constraint(weights, pltpu.VMEM)
    right_a, left_b = z_step(far_a, 1), z_step(far_b, -1)
    sums = partial_sums((far_a,), 3, 5)
    right_b, left_a = z_step(sums[1], 1), z_step(sums[2], -1)
    right_a, left_b = plus(right_a, sums[0]), plus(left_b, sums[3])
    for near in (2, 1):
        sums = partial_sums((right_a, left_b), near, 8 - near)
        right_a, left_b = z_step(right_a, 1), z_step(left_b, -1)
        right_b, left_a = plus(right_b, sums[1]), plus(left_a, sums[2])
        right_b, left_a = z_step(right_b, 1), z_step(left_a, -1)
        right_a, left_b = plus(right_a, sums[0]), plus(left_b, sums[3])
    own_a, own_b, after = partial_sums((right_a, left_b), 0, with_after=True)
    right_a, left_b = z_step(right_a, 1), z_step(left_b, -1)
    wide = lambda v: v.astype(F32)
    mlp_sum = jnp.concatenate(
        [wide(own_a) + wide(right_a) + wide(left_a), wide(own_b) + wide(right_b) + wide(left_b)], axis=0
    )
    return (wide(after) + mlp_sum).astype(BF16)


def solution(mesh):
    placed = (
        P(AXES, None),
        P(AXES, None),
        P(AXES, None),
        P(),
        P(),
        P(),
        P("inner", "outer"),
        P("inner", "outer"),
        P("outer", "inner"),
    )
    return jax.shard_map(
        per_device,
        mesh=mesh,
        in_specs=placed,
        out_specs=P(AXES, None),
        check_vma=False,
    )
```

```python
import functools

import jax
import jax.numpy as jnp
from jax import lax
from jax.experimental import pallas as pl
from jax.experimental.pallas import tpu as pltpu
from jax.sharding import PartitionSpec as P

HD = 128
QHEADS = 2
SPAN = 64
AXES = ("outer", "inner")
F32 = jnp.float32
BF16 = jnp.bfloat16


def device_at(z, x, y, core):
    return ((z * 2 + x // 2) * 2 + x % 2) * 8 + y * 2 + core


def places():
    return [(z, x, y, core) for z in range(8) for x in range(4) for y in range(4) for core in range(2)]


def send(array, target):
    return lax.ppermute(array, AXES, [(device_at(*p), device_at(*target(*p))) for p in places()])


def z_step(array, distance):
    return send(array, lambda z, x, y, core: ((z + distance) % 8, x, y, core))


def from_y(array, distance):
    return send(array, lambda z, x, y, core: (z, x, (y - distance) % 4, core))


def other_core(array):
    return send(array, lambda z, x, y, core: (z, x, y, 1 - core))


def from_block(array, back, other_x):
    def target(z, x, y, core):
        block = (z * 2 + x // 2 + back) % 16
        return (block // 2, block % 2 * 2 + (x % 2 ^ other_x), y, core)

    return send(array, target)


def attention_kernel(place_ref, order_ref, q_ref, *refs):
    kv_refs, out_ref = refs[:-1], refs[-1]
    rows = q_ref.shape[0]
    outer, inner = place_ref[0], place_ref[1]
    x_lo, y, core = inner // 8, lax.rem(inner // 2, 4), lax.rem(inner, 2)
    q = jnp.concatenate([q_ref[:, :HD], q_ref[:, HD:]], axis=0)

    def positions(member, dim):
        shape = (1, rows) if dim else (rows, 1)
        r = lax.broadcasted_iota(jnp.int32, shape, dim)
        return jnp.where(
            r < SPAN, order_ref[2 * member] * SPAN + r, order_ref[2 * member + 1] * SPAN + r - SPAN
        )

    qpos = positions(inner, 0)
    qpos = jnp.concatenate([qpos, qpos], axis=0)
    kpos, own, before = [], [], []
    for from_core in range(2):
        for step in range(4):
            block = kv_refs[4 * from_core + step]
            for other_x in range(2):
                member = (
                    lax.rem(x_lo + other_x, 2) * 8 + lax.rem(y + step, 4) * 2 + lax.rem(core + from_core, 2)
                )
                kpos.append(positions(member, 1))
                own.append(block[:, 4 * HD * other_x : 4 * HD * other_x + 2 * HD])
                before.append(block[:, 4 * HD * other_x + 2 * HD : 4 * HD * (other_x + 1)])
    kpos = jnp.concatenate(kpos, axis=1)
    own, before = jnp.concatenate(own, axis=0), jnp.concatenate(before, axis=0)
    contract = (((1,), (1,)), ((), ()))
    scale = HD ** (-0.5)
    own_score = lax.dot_general(q, own[:, :HD], contract, preferred_element_type=F32) * scale
    before_score = lax.dot_general(q, before[:, :HD], contract, preferred_element_type=F32) * scale
    own_seen = kpos <= qpos
    before_seen = jnp.broadcast_to(outer > 0, before_score.shape)
    own_score = jnp.where(own_seen, own_score, -1e30)
    before_score = jnp.where(before_seen, before_score, -1e30)
    top = jnp.maximum(
        jnp.max(own_score, axis=1, keepdims=True), jnp.max(before_score, axis=1, keepdims=True)
    )
    own_weight = jnp.where(own_seen, jnp.exp(own_score - top), 0.0)
    before_weight = jnp.where(before_seen, jnp.exp(before_score - top), 0.0)
    total = jnp.sum(own_weight, axis=1, keepdims=True) + jnp.sum(before_weight, axis=1, keepdims=True)
    mixed = jnp.dot(own_weight.astype(BF16), own[:, HD:], preferred_element_type=F32)
    mixed = mixed + jnp.dot(before_weight.astype(BF16), before[:, HD:], preferred_element_type=F32)
    attended = (mixed / total).astype(BF16)
    attended = jnp.concatenate([attended[:rows], attended[rows:]], axis=1)
    for copy in range(out_ref.shape[0]):
        out_ref[copy] = attended


def shard_kernel(gate_ref, up_ref, down_ref, out_ref):
    wide = gate_ref.shape[0] // HD
    tiles = [ref[HD * t : HD * (t + 1)] for ref in (gate_ref, up_ref) for t in range(wide)]
    tiles.append(jnp.concatenate([gate_ref[HD * wide :], up_ref[HD * wide :]], axis=0))
    for t, tile in enumerate(tiles):
        out_ref[HD * t : HD * (t + 1)] = tile.astype(F32).T.astype(BF16)
    out_ref[HD * len(tiles) :] = down_ref[...]


def mlp_kernel(
    distances, resid_counts, with_after, loads, place_ref, att_ref, proj_ref, gain_ref, weight_ref, *refs
):
    copies = []
    if loads:
        source, weight_ref, sems = weight_ref, refs[-2], refs[-1]
        split = weight_ref.shape[1] // 3 * 2
        for n, x_hi in enumerate((0, 1)):
            for k, rows in enumerate((pl.ds(0, split), pl.ds(split, split // 2))):
                part = (pl.ds(16 * x_hi, 16), rows)
                copies.append(pltpu.make_async_copy(source.at[part], weight_ref.at[part], sems.at[2 * n + k]))
        for copy in copies:
            copy.start()
    inputs = sum(resid_counts)
    resid_refs, refs = refs[:inputs], refs[inputs:]
    out_refs = refs[: 2 * len(distances)]
    z = place_ref[0] // 2
    normed, first = [], 0
    for distance, pieces in zip(distances, resid_counts):
        resid = jnp.concatenate([r[...] for r in resid_refs[first : first + pieces]], axis=0)
        first += pieces
        mixed = jnp.dot(
            att_ref[lax.rem(z + distance, 8)], proj_ref[...], preferred_element_type=F32
        )
        after = (resid.astype(F32) + mixed).astype(BF16)
        if with_after:
            refs[-1][...] = after
        wide = after.astype(F32)
        scale = lax.rsqrt(jnp.mean(wide * wide, axis=1, keepdims=True) + 1e-05)
        normed.append((wide * scale * gain_ref[...]).astype(BF16))
    normed = jnp.concatenate(normed, axis=0)
    total = None
    units = weight_ref.shape[1] // 3
    wide_units = units // HD * HD
    for x_hi in range(2):
        members = slice(16 * x_hi, 16 * x_hi + 16)
        if loads:
            copies[2 * x_hi].wait()
        columns = [
            weight_ref[members, HD * tile : HD * (tile + 1), :].reshape(16 * HD, HD)
            for tile in range(2 * units // HD)
        ]
        both = jnp.dot(normed, jnp.concatenate(columns, axis=1), preferred_element_type=F32)
        gate, upward, last = (
            both[:, :wide_units],
            both[:, wide_units : 2 * wide_units],
            both[:, 2 * wide_units :],
        )
        silu = lambda v: v / (1.0 + jnp.exp(-v))
        last = silu(last) * pltpu.roll(last, HD // 2, 1)
        hidden = jnp.concatenate([silu(gate) * upward, last[:, : HD // 2]], axis=1).astype(BF16)
        if loads:
            copies[2 * x_hi + 1].wait()
        down = jnp.concatenate(
            [weight_ref[16 * x_hi + m, 2 * units :, :] for m in range(16)], axis=1
        )
        term = jnp.dot(hidden, down, preferred_element_type=F32)
        total = term if total is None else total + term
    final = total.astype(BF16)
    half = out_refs[0].shape[0]
    for n, ref in enumerate(out_refs):
        ref[...] = final[half * n : half * (n + 1)]


def mlp_part(distances, place, resid_pieces, att_all, out_proj, gain, weights, with_after=False, loads=False):
    width = gain.shape[1]
    rows = att_all.shape[1]
    piece = jax.ShapeDtypeStruct((rows // 2, width), BF16)
    out_shape = [piece] * (2 * len(distances))
    if with_after:
        out_shape = out_shape + [jax.ShapeDtypeStruct((rows, width), BF16)]
    scratch = []
    if loads:
        out_shape = out_shape + [pltpu.VMEM(weights.shape, BF16)]
        scratch = [pltpu.SemaphoreType.DMA((4,))]
    vmem = pl.BlockSpec(memory_space=pltpu.VMEM)
    pieces = [p for some in resid_pieces for p in some]
    count = rows * len(distances)
    return pl.pallas_call(
        functools.partial(mlp_kernel, distances, [len(some) for some in resid_pieces], with_after, loads),
        out_shape=out_shape,
        in_specs=[pl.BlockSpec(memory_space=pltpu.SMEM)]
        + [vmem] * 3
        + [pl.BlockSpec(memory_space=pl.ANY) if loads else vmem]
        + [vmem] * len(pieces),
        out_specs=[vmem] * len(out_shape),
        scratch_shapes=scratch,
        compiler_params=pltpu.CompilerParams(vmem_limit_bytes=32 * 1024 * 1024),
        cost_estimate=pl.CostEstimate(
            flops=2 * count * weights.size, bytes_accessed=weights.size * 2, transcendentals=count * 1024
        ),
        name=f"mlp_{len(distances)}_{distances[0]}",
    )(place, att_all, out_proj, gain, weights, *pieces)


def per_device(resid, queries, keyvals, piece_order, out_proj, mlp_gain, w_gate, w_up, w_down):
    rows, width = resid.shape
    half = rows // 2
    place = jnp.stack([lax.axis_index("outer"), lax.axis_index("inner")]).astype(jnp.int32)

    shard = pl.pallas_call(
        shard_kernel,
        out_shape=jax.ShapeDtypeStruct((3 * w_down.shape[0], HD), BF16),
        in_specs=[pl.BlockSpec(memory_space=pltpu.VMEM)] * 3,
        out_specs=pl.BlockSpec(memory_space=pltpu.VMEM),
        name="shard",
    )(w_gate.T, w_up.T, w_down)
    planes = [[z * 32 + member for member in range(32)] for z in range(8)]
    weights = lax.all_gather(shard, AXES, axis_index_groups=planes, axis=0)

    across_x = jnp.concatenate(
        [keyvals, from_block(keyvals, 1, 0), from_block(keyvals, 0, 1), from_block(keyvals, 1, 1)], axis=1
    )
    pieces = {0: [resid]}
    ring_start = lax.optimization_barrier((resid, across_x))[0]
    right, left = z_step(ring_start, 1), z_step(ring_start, -1)
    pieces[7], pieces[1] = [right], [left]
    own_kv = [across_x] + [from_y(across_x, step) for step in (1, 2, 3)]
    next_right, next_left = lax.optimization_barrier((right, left, own_kv[3]))[:2]
    pieces[7], pieces[1] = [right], [left]
    right, left = z_step(next_right, 1), z_step(next_left, -1)
    far = jnp.concatenate(own_kv[1:], axis=0)
    pieces[6], pieces[2] = [right], [left]
    far = other_core(far)
    sib_kv = [other_core(across_x)] + [far[rows * n : rows * (n + 1)] for n in range(3)]
    attended = pl.pallas_call(
        attention_kernel,
        out_shape=jax.ShapeDtypeStruct((8, rows, QHEADS * HD), BF16),
        in_specs=[pl.BlockSpec(memory_space=pltpu.SMEM)] * 2
        + [pl.BlockSpec(memory_space=pltpu.VMEM)] * 9,
        out_specs=pl.BlockSpec(memory_space=pltpu.VMEM),
        compiler_params=pltpu.CompilerParams(vmem_limit_bytes=32 * 1024 * 1024),
        cost_estimate=pl.CostEstimate(
            flops=4 * 2 * rows * 32 * rows * HD, bytes_accessed=3 * 2**20, transcendentals=2 * rows * 32 * rows
        ),
        name="attention",
    )(place, piece_order, queries, *own_kv, *sib_kv)
    attended = lax.optimization_barrier((attended, right, left))[0]
    right_a, left_b = z_step(right[:half], 1), z_step(left[half:], -1)
    pieces[4] = [z_step(right_a, 1), z_step(left_b, -1)]
    z_groups = [[z * 2 + x_hi for z in range(8)] for x_hi in range(2)]
    att_all = lax.all_to_all(attended, "outer", 0, 0, axis_index_groups=z_groups, tiled=True)

    late = lax.optimization_barrier((right[half:], left[:half], att_all))
    pieces[5] = [right_a, z_step(late[0], 1)]
    pieces[3] = [z_step(late[1], -1), left_b]

    gain = mlp_gain.reshape(1, width)

    def partial_sums(after, *distances, with_after=False, loads=False):
        ready = lax.optimization_barrier((att_all,) + after)[0]
        return mlp_part(
            distances, place, [pieces[d] for d in distances], ready, out_proj, gain, weights, with_after, loads
        )

    plus = lambda u, v: (u.astype(F32) + v.astype(F32)).astype(BF16)
    far_a, far_b, weights = partial_sums((), 4, loads=True)
    weights = pltpu.with_memory_space_constraint(weights, pltpu.VMEM)
    right_a, left_b = z_step(far_a, 1), z_step(far_b, -1)
    sums = partial_sums((far_a,), 3, 5)
    right_b, left_a = z_step(sums[1], 1), z_step(sums[2], -1)
    right_a, left_b = plus(right_a, sums[0]), plus(left_b, sums[3])
    for near in (2, 1):
        sums = partial_sums((right_a, left_b), near, 8 - near)
        right_a, left_b = z_step(right_a, 1), z_step(left_b, -1)
        right_b, left_a = plus(right_b, sums[1]), plus(left_a, sums[2])
        right_b, left_a = z_step(right_b, 1), z_step(left_a, -1)
        right_a, left_b = plus(right_a, sums[0]), plus(left_b, sums[3])
    own_a, own_b, after = partial_sums((right_a, left_b), 0, with_after=True)
    right_a, left_b = z_step(right_a, 1), z_step(left_b, -1)
    wide = lambda v: v.astype(F32)
    mlp_sum = jnp.concatenate(
        [wide(own_a) + wide(right_a) + wide(left_a), wide(own_b) + wide(right_b) + wide(left_b)], axis=0
    )
    return (wide(after) + mlp_sum).astype(BF16)


def solution(mesh):
    placed = (
        P(AXES, None),
        P(AXES, None),
        P(AXES, None),
        P(),
        P(),
        P(),
        P("inner", "outer"),
        P("inner", "outer"),
        P("outer", "inner"),
    )
    return jax.shard_map(
        per_device,
        mesh=mesh,
        in_specs=placed,
        out_specs=P(AXES, None),
        check_vma=False,
    )
```
